128 devices in a mesh: gx: 32 (over y, x, core), gz: 4 (over z).
Axes of the slice: x: 4, y: 4, z: 4, core: 2. Of those that a mesh axis runs over, the one named last changes fastest.
Arguments:
- features: float32 [4, 1024, 128, 512], P(None, 'gx', None, 'gz'), may hold values from -6 to 6
- w_in: float32 [16, 4], replicated, may hold values from -3 to 3
- b_in: float32 [16], replicated, may hold values from -3 to 3
- w_out: float32 [12, 16], replicated, may hold values from -1.5 to 1.5
- b_out: float32 [12], replicated, may hold values from -4 to 4
- band_depth: float32 [8], replicated, may hold values from 0.5 to 20
- band_mix: float32 [3, 8], replicated, may hold values from 0.05 to 0.3
Outputs:
- light: float32 [3, 1024, 128, 512], P(None, 'gx', None, 'gz')
- image: float32 [4, 1024, 128], P(None, 'gx', 'gz')
The draws below stay inside these ranges and needn't reach their ends.
All inputs are finite; a program needn't handle non-finite values.
Results may differ from the reference program's by a relative error of at most 0.0003.
Values sent between devices are 32-bit elements; how exact they have to be, the bound alone decides.
No kernel may reach another device: no remote copies, remote signals or barrier semaphores. Data moves between devices by JAX's collectives and lax.ppermute only.
A program may use at most 192 MiB of HBM per device.

```python
import math
import jax
import jax.numpy as jnp
from jax import lax

CHANNELS = 4
UNITS = 16
BANDS = 8
NY = 128
NX = 1024
NZ = 512


def shard_levels(stream_key, extent, shards, smallest, largest):
    def one(position, blocks):
        steps = jax.random.uniform(jax.random.fold_in(jax.random.fold_in(stream_key, 6), position), (blocks,), jnp.float32, smallest / len(shards), largest / len(shards))
        return jnp.repeat(jnp.exp(steps), extent[position] // blocks).reshape((-1,) + (1,) * (len(extent) - position - 1))

    loudness = one(*shards[0])
    for cut in shards[1:]:
        loudness = loudness * one(*cut)
    return loudness


def normal_values(rng, dims, width, limit, split=(), dtype=jnp.bfloat16):
    drawn = jax.random.normal(rng, dims, jnp.float32) * width
    if len(split) > 0:
        drawn = shard_levels(rng, dims, split, -0.22, 0.18) * drawn
    return jnp.clip(drawn, min=-limit, max=limit).astype(dtype)


def setup_inputs(seed: int = 0) -> dict:
    key_of = jax.random.split(jax.random.key(seed), 8)
    features = normal_values(key_of[0], (CHANNELS, NX, NY, NZ), 1.0, 6.0, ((1, 32), (3, 4)), jnp.float32)
    w_in = normal_values(key_of[1], (UNITS, CHANNELS), CHANNELS ** -0.5, 3.0, (), jnp.float32)
    b_in = normal_values(key_of[2], (UNITS,), 0.5, 3.0, (), jnp.float32)
    w_out = normal_values(key_of[3], (BANDS + 4, UNITS), UNITS ** -0.5, 1.5, (), jnp.float32)
    b_out = normal_values(key_of[4], (BANDS + 4,), 1.0, 4.0, (), jnp.float32)
    band_depth = jnp.clip(jnp.exp(jax.random.uniform(key_of[5], (BANDS,), jnp.float32, math.log(0.5), math.log(20.0))), 0.5, 20.0)
    band_mix = jnp.clip(jax.random.uniform(key_of[6], (3, BANDS), jnp.float32, 0.05, 0.3), 0.05, 0.3)
    return {"features": features, "w_in": w_in, "b_in": b_in, "w_out": w_out, "b_out": b_out, "band_depth": band_depth, "band_mix": band_mix}


def reference(features, w_in, b_in, w_out, b_out, band_depth, band_mix):
    high = lax.Precision.HIGHEST

    def advance(shadow, plane):
        hidden = jax.nn.relu(jnp.einsum("hc,cyz->hyz", w_in, plane, precision=high) + b_in[:, None, None])
        raw = jnp.einsum("oh,hyz->oyz", w_out, hidden, precision=high) + b_out[:, None, None]
        extinction = jax.nn.softplus(raw[:BANDS]) * (band_depth / NX)[:, None, None]
        light = jax.nn.sigmoid(raw[BANDS:BANDS + 3]) * jnp.einsum("kb,byz->kyz", band_mix, jnp.exp(-shadow), precision=high)
        kappa = jax.nn.softplus(raw[BANDS + 3]) / NZ
        occlusion = jnp.cumsum(kappa, axis=1) - kappa
        weight = jnp.exp(-occlusion) * (1.0 - jnp.exp(-kappa))
        colour = jnp.sum(light * weight[None], axis=2)
        alpha = 1.0 - jnp.exp(-jnp.sum(kappa, axis=1))
        return shadow + extinction, (light, jnp.concatenate([colour, alpha[None]], axis=0))

    start = jnp.zeros((BANDS, NY, NZ), jnp.float32)
    final, (lights, pixels) = lax.scan(advance, start, jnp.moveaxis(features, 1, 0))
    return jnp.moveaxis(lights, 0, 1), jnp.moveaxis(pixels, 0, 1)
```

```python
import functools
import math

import jax
import jax.numpy as jnp
from jax import lax
from jax.experimental import pallas as pl
from jax.experimental.pallas import tpu as pltpu
from jax.sharding import PartitionSpec as P

BANDS = 8
UNITS = 16
FEATS = 4
OUTS = 12
SLAB = 16
LOG2E = math.log2(math.e)
F32 = jnp.float32
BF16 = jnp.bfloat16


def iota(shape, dim):
    return lax.broadcasted_iota(jnp.int32, shape, dim)


def split(value):
    high = value.astype(BF16)
    return high, (value - high.astype(F32)).astype(BF16)


def exact_dot(a, b):
    return jnp.dot(a, b, precision=lax.Precision.HIGHEST, preferred_element_type=F32)


def one_hot(shape, condition):
    return jnp.where(condition, jnp.ones(shape, F32), jnp.zeros(shape, F32))


def bias_columns(column):
    rows = column.shape[0]
    high = column.astype(BF16).astype(F32)
    rest = column - high
    middle = rest.astype(BF16).astype(F32)
    low = rest - middle
    lane = iota((rows, 16), 1)
    zero = jnp.zeros((rows, 16), F32)
    return jnp.where(
        lane == 0, high, jnp.where(lane == 1, middle, jnp.where(lane == 2, low, zero))
    ).astype(BF16)


def build_first(w_in, b_in):
    rows, cols = SLAB * UNITS, FEATS * SLAB
    pick = one_hot((rows, UNITS), iota((rows, UNITS), 0) % UNITS == iota((rows, UNITS), 1))
    spread = one_hot((FEATS, cols), iota((FEATS, cols), 1) // SLAB == iota((FEATS, cols), 0))
    full = exact_dot(exact_dot(pick, w_in), spread)
    full = jnp.where(iota((rows, cols), 0) // UNITS == iota((rows, cols), 1) % SLAB, full, 0.0)
    high, low = split(full)
    bias = bias_columns(jnp.sum(pick * b_in, axis=1, keepdims=True))
    return high, low, bias


def build_second(w_out, b_out):
    rows, cols = OUTS * 8, 8 * UNITS
    pick = one_hot((rows, OUTS), iota((rows, OUTS), 0) // 8 == iota((rows, OUTS), 1))
    spread = one_hot((UNITS, cols), iota((UNITS, cols), 1) % UNITS == iota((UNITS, cols), 0))
    full = exact_dot(exact_dot(pick, w_out), spread)
    full = jnp.where(iota((rows, cols), 0) % 8 == iota((rows, cols), 1) // UNITS, full, 0.0)
    out = iota((rows, 1), 0) // 8
    scale = jnp.where((out >= BANDS) & (out < BANDS + 3), -LOG2E, 1.0)
    high, low = split(full * scale)
    bias = bias_columns(jnp.sum(pick * b_out, axis=1, keepdims=True) * scale)
    return high, low, bias


def softplus(x):
    return jnp.maximum(jnp.log(1.0 + jnp.exp(jnp.minimum(x, 80.0))), x)


def front_kernel(total_x, total_z, unroll, f_ref, win_ref, bin_ref, wout_ref, bout_ref, depth_ref,
                 mid_ref, sum_ref, dep_ref, first_ref, second_ref, tri_ref, kap_ref):
    cells_x = f_ref.shape[1]
    step = pl.program_id(0)

    @pl.when(step == 0)
    def _():
        high, low, bias = build_first(win_ref[...], bin_ref[...])
        first_ref[:, 0:64] = high
        first_ref[:, 64:128] = high
        first_ref[:, 128:192] = low
        first_ref[:, 192:208] = bias
        high, low, bias = build_second(wout_ref[...], bout_ref[...])
        second_ref[:, 0:128] = high
        second_ref[:, 128:256] = high
        second_ref[:, 256:384] = low
        second_ref[:, 384:400] = bias
        tri_ref[...] = one_hot((256, 128), iota((256, 128), 0) % 128 < iota((256, 128), 1)).astype(BF16)

    ones = jnp.ones((16, 256), BF16)
    rates = [depth_ref[b] * (-LOG2E / total_x) for b in range(BANDS)]
    fade = -LOG2E / total_z
    y0 = pl.multiple_of(step * SLAB, SLAB)

    def pair(i, sums):
        sums = list(sums)
        x0 = 2 * i
        rows = jnp.concatenate(
            [jnp.concatenate([f_ref[c, x0], f_ref[c, x0 + 1]], axis=1) for c in range(FEATS)], axis=0
        )
        high, low = split(rows)
        hidden = jnp.dot(first_ref[...], jnp.concatenate([high, low, high, ones], axis=0),
                         preferred_element_type=F32)
        high, low = split(jnp.maximum(hidden, 0.0))
        for j in range(2):
            part = slice(j * 128, j * 128 + 128)
            raw = jnp.dot(second_ref[...],
                          jnp.concatenate([high[part], low[part], high[part], ones], axis=0),
                          preferred_element_type=F32)
            here = pl.ds(pl.multiple_of(y0 + 8 * j, 8), 8)
            for s in range(2):
                x = x0 + s
                tile = raw[:, s * 128 : s * 128 + 128]
                for b in range(BANDS):
                    total = sums[j * BANDS + b]
                    mid_ref[b, x, here, :] = jnp.exp2(total * rates[b])
                    sums[j * BANDS + b] = total + softplus(tile[8 * b : 8 * b + 8])
                for k in range(BANDS, BANDS + 3):
                    mid_ref[k, x, here, :] = pl.reciprocal(
                        1.0 + jnp.exp2(tile[8 * k : 8 * k + 8]), approx=True)
                kappa = softplus(tile[8 * BANDS + 24 : 8 * BANDS + 32])
                high_k, low_k = split(kappa)
                both = jnp.concatenate([high_k, low_k], axis=1)
                occlusion = jnp.dot(both, tri_ref[...], preferred_element_type=F32)
                mid_ref[BANDS + 3, x, here, :] = jnp.exp2(occlusion * fade) * (1.0 - jnp.exp2(kappa * fade))
                kap_ref[j, pl.ds(pl.multiple_of(x * 8, 8), 8), :] = jnp.concatenate(
                    [high_k.astype(F32), low_k.astype(F32)], axis=1)
        return tuple(sums)

    zero = jnp.zeros((8, 128), F32)
    sums = lax.fori_loop(0, cells_x // 2, pair, (zero,) * (2 * BANDS), unroll=unroll)
    for j in range(2):
        for b in range(BANDS):
            sum_ref[b, 8 * j : 8 * j + 8, :] = sums[j * BANDS + b]
        select = one_hot((8, 256), iota((8, 256), 0) == 3).astype(BF16)
        dep_ref[j] = lax.dot_general(select, kap_ref[j].astype(BF16), (((1,), (1,)), ((), ())),
                                     preferred_element_type=F32) * (1.0 / total_z)


def back_kernel(total_x, unroll, mid_ref, inc_ref, dep_ref, depth_ref, mix_ref,
                light_ref, img_ref, prod_ref):
    cells_x = light_ref.shape[1]
    gains = []
    for b in range(BANDS):
        fade = jnp.exp2(inc_ref[b] * (depth_ref[b] * (-LOG2E / total_x)))
        gains.append([fade * mix_ref[k * BANDS + b] for k in range(3)])

    def one(x, carry):
        bands = [mid_ref[b, x] for b in range(BANDS)]
        weight = mid_ref[BANDS + 3, x]
        for k in range(3):
            total = bands[0] * gains[0][k]
            for b in range(1, BANDS):
                total = total + bands[b] * gains[b][k]
            light = total * mid_ref[BANDS + k, x]
            light_ref[k, x] = light
            high, low = split(light * weight)
            here = pl.ds(pl.multiple_of(x * 8, 8), 8)
            prod_ref[here, 256 * k : 256 * k + 128] = high.astype(F32)
            prod_ref[here, 256 * k + 128 : 256 * k + 256] = low.astype(F32)
        return carry

    lax.fori_loop(0, cells_x, one, 0, unroll=unroll)
    select = one_hot((8, 768), iota((8, 768), 0) == iota((8, 768), 1) // 256).astype(BF16)
    img_ref[0] = lax.dot_general(select, prod_ref[...].astype(BF16), (((1,), (1,)), ((), ())),
                                 preferred_element_type=F32) + dep_ref[0]


def front(features, w_in, b_in, w_out, b_out, band_depth, total_x, total_z):
    _, cells_x, rows_y, cells_z = features.shape
    whole = pl.BlockSpec(memory_space=pltpu.VMEM)
    return pl.pallas_call(
        functools.partial(front_kernel, total_x, total_z, 2),
        grid=(rows_y // SLAB,),
        in_specs=[
            pl.BlockSpec((FEATS, cells_x, SLAB, cells_z), lambda i: (0, 0, i, 0)),
            whole, whole, whole, whole,
            pl.BlockSpec(memory_space=pltpu.SMEM),
        ],
        out_specs=[
            whole,
            pl.BlockSpec((BANDS, SLAB, cells_z), lambda i: (0, i, 0)),
            pl.BlockSpec((2, 8, 256), lambda i: (i, 0, 0)),
        ],
        out_shape=[
            pltpu.MemorySpace.VMEM((OUTS, cells_x, rows_y, cells_z), F32),
            jax.ShapeDtypeStruct((BANDS, rows_y, cells_z), F32),
            jax.ShapeDtypeStruct((rows_y // 8, 8, 256), F32),
        ],
        scratch_shapes=[
            pltpu.VMEM((SLAB * UNITS, 208), BF16),
            pltpu.VMEM((OUTS * 8, 400), BF16),
            pltpu.VMEM((256, 128), BF16),
            pltpu.VMEM((2, 256, 256), F32),
        ],
        compiler_params=pltpu.CompilerParams(vmem_limit_bytes=24 << 20),
        name="front",
    )(features, w_in, b_in[None], w_out, b_out[None], band_depth)


def back(mid, incoming, dep, band_depth, band_mix, total_x):
    _, cells_x, rows_y, cells_z = mid.shape
    return pl.pallas_call(
        functools.partial(back_kernel, total_x, 4),
        grid=(rows_y // 8,),
        in_specs=[
            pl.BlockSpec((OUTS, cells_x, 8, cells_z), lambda i: (0, 0, i, 0)),
            pl.BlockSpec((BANDS, 8, cells_z), lambda i: (0, i, 0)),
            pl.BlockSpec((1, 8, 256), lambda i: (i, 0, 0)),
            pl.BlockSpec(memory_space=pltpu.SMEM),
            pl.BlockSpec(memory_space=pltpu.SMEM),
        ],
        out_specs=[
            pl.BlockSpec((3, cells_x, 8, cells_z), lambda i: (0, 0, i, 0)),
            pl.BlockSpec((1, 8, 256), lambda i: (i, 0, 0)),
        ],
        out_shape=[
            jax.ShapeDtypeStruct((3, cells_x, rows_y, cells_z), F32),
            jax.ShapeDtypeStruct((rows_y // 8, 8, 256), F32),
        ],
        scratch_shapes=[pltpu.VMEM((256, 768), F32)],
        compiler_params=pltpu.CompilerParams(vmem_limit_bytes=24 << 20),
        name="back",
    )(mid, incoming, dep, band_depth, band_mix.reshape(-1))


def scan_x(total):
    count = lax.axis_size("gx")
    pieces = total.reshape(count, -1, total.shape[-1])
    pieces = lax.all_to_all(pieces, "gx", 0, 0, tiled=True)
    pieces = jnp.cumsum(pieces, axis=0) - pieces
    pieces = lax.all_to_all(pieces, "gx", 0, 0, tiled=True)
    return pieces.reshape(total.shape)


def composite(parts, cells_x):
    ndev = lax.axis_size("gz")
    me = lax.axis_index("gz")
    slabs = parts.shape[0]
    parts = parts.reshape(ndev, slabs // ndev, 8, parts.shape[-1])
    held = []
    for apart in range(ndev):
        piece = lax.dynamic_index_in_dim(parts, (me + apart) % ndev, 0, keepdims=False)[:, :4]
        if apart:
            piece = lax.ppermute(piece, "gz", [(i, (i + apart) % ndev) for i in range(ndev)])
        held.append((piece, (me - apart) % ndev))
    colour = 0.0
    depth = 0.0
    for piece, source in held:
        ahead = 0.0
        for other, origin in held:
            if other is not piece:
                ahead = ahead + jnp.where(origin < source, other[:, 3:], 0.0)
        colour = colour + jnp.exp(-ahead) * piece[:, :3]
        depth = depth + piece[:, 3:]
    image = jnp.concatenate([colour, 1.0 - jnp.exp(-depth)], axis=1)
    image = image.reshape(slabs // ndev, 4, cells_x, 8)
    return image.transpose(1, 2, 0, 3).reshape(4, cells_x, slabs // ndev * 8)


def body(features, w_in, b_in, w_out, b_out, band_depth, band_mix):
    cells_x = features.shape[1]
    total_x = cells_x * lax.axis_size("gx")
    total_z = features.shape[3] * lax.axis_size("gz")
    mid, total, dep = front(features, w_in, b_in, w_out, b_out, band_depth, total_x, total_z)
    incoming = scan_x(total)
    light, parts = back(mid, incoming, dep, band_depth, band_mix, total_x)
    return light, composite(parts, cells_x)


def solution(mesh):
    in_specs = (P(None, "gx", None, "gz"), P(), P(), P(), P(), P(), P())
    out_specs = (P(None, "gx", None, "gz"), P(None, "gx", "gz"))
    return jax.shard_map(body, mesh=mesh, in_specs=in_specs, out_specs=out_specs, check_vma=False)
```

```python
import functools
import math

import jax
import jax.numpy as jnp
from jax import lax
from jax.experimental import pallas as pl
from jax.experimental.pallas import tpu as pltpu
from jax.sharding import PartitionSpec as P

BANDS = 8
UNITS = 16
FEATS = 4
OUTS = 12
SLAB = 16
CHUNKS = 1
LOG2E = math.log2(math.e)
F32 = jnp.float32
BF16 = jnp.bfloat16


def iota(shape, dim):
    return lax.broadcasted_iota(jnp.int32, shape, dim)


def split(value):
    high = value.astype(BF16)
    return high, (value - high.astype(F32)).astype(BF16)


def exact_dot(a, b):
    return jnp.dot(a, b, precision=lax.Precision.HIGHEST, preferred_element_type=F32)


def one_hot(shape, condition):
    return jnp.where(condition, jnp.ones(shape, F32), jnp.zeros(shape, F32))


def bias_columns(column):
    rows = column.shape[0]
    high = column.astype(BF16).astype(F32)
    rest = column - high
    middle = rest.astype(BF16).astype(F32)
    low = rest - middle
    lane = iota((rows, 16), 1)
    zero = jnp.zeros((rows, 16), F32)
    return jnp.where(
        lane == 0, high, jnp.where(lane == 1, middle, jnp.where(lane == 2, low, zero))
    ).astype(BF16)


def build_first(w_in, b_in):
    rows, cols = SLAB * UNITS, FEATS * SLAB
    pick = one_hot((rows, UNITS), iota((rows, UNITS), 0) % UNITS == iota((rows, UNITS), 1))
    spread = one_hot((FEATS, cols), iota((FEATS, cols), 1) // SLAB == iota((FEATS, cols), 0))
    full = exact_dot(exact_dot(pick, w_in), spread)
    full = jnp.where(iota((rows, cols), 0) // UNITS == iota((rows, cols), 1) % SLAB, full, 0.0)
    high, low = split(full)
    bias = bias_columns(jnp.sum(pick * b_in, axis=1, keepdims=True))
    return high, low, bias


def build_second(w_out, b_out):
    rows, cols = OUTS * 8, 8 * UNITS
    pick = one_hot((rows, OUTS), iota((rows, OUTS), 0) // 8 == iota((rows, OUTS), 1))
    spread = one_hot((UNITS, cols), iota((UNITS, cols), 1) % UNITS == iota((UNITS, cols), 0))
    full = exact_dot(exact_dot(pick, w_out), spread)
    full = jnp.where(iota((rows, cols), 0) % 8 == iota((rows, cols), 1) // UNITS, full, 0.0)
    out = iota((rows, 1), 0) // 8
    scale = jnp.where((out >= BANDS) & (out < BANDS + 3), -LOG2E, 1.0)
    high, low = split(full * scale)
    bias = bias_columns(jnp.sum(pick * b_out, axis=1, keepdims=True) * scale)
    return high, low, bias


def softplus(x):
    return jnp.maximum(jnp.log(1.0 + jnp.exp(jnp.minimum(x, 80.0))), x)


def front_kernel(total_x, total_z, batch, unroll, f_ref, win_ref, bin_ref, wout_ref, bout_ref, depth_ref,
                 mid_ref, sum_ref, dep_ref, first_ref, second_ref, tri_ref):
    cells_x = f_ref.shape[1]
    step = pl.program_id(0)

    @pl.when(step == 0)
    def _():
        high, low, bias = build_first(win_ref[...].T, bin_ref[...])
        first_ref[:, 0:64] = high
        first_ref[:, 64:128] = high
        first_ref[:, 128:192] = low
        first_ref[:, 192:208] = bias
        high, low, bias = build_second(wout_ref[...], bout_ref[...])
        second_ref[:, 0:128] = high
        second_ref[:, 128:256] = high
        second_ref[:, 256:384] = low
        second_ref[:, 384:400] = bias
        tri_ref[...] = one_hot((256, 128), iota((256, 128), 0) % 128 < iota((256, 128), 1)).astype(BF16)

    ones = jnp.ones((16, 128 * batch), BF16)
    rates = [depth_ref[b] * (-LOG2E / total_x) for b in range(BANDS)]
    fade = -LOG2E / total_z

    def layer_one(x0):
        rows = jnp.concatenate(
            [jnp.concatenate([f_ref[c, x0 + s] for s in range(batch)], axis=1) for c in range(FEATS)], axis=0
        )
        high, low = split(rows)
        return jnp.dot(first_ref[...], jnp.concatenate([high, low, high, ones], axis=0),
                       preferred_element_type=F32)

    def layer_two(hidden):
        high, low = split(jnp.maximum(hidden, 0.0))
        raws = []
        for j in range(2):
            part = slice(j * 128, j * 128 + 128)
            raws.append(jnp.dot(second_ref[...],
                                jnp.concatenate([high[part], low[part], high[part], ones], axis=0),
                                preferred_element_type=F32))
        return raws

    def finish(x0, raws, sums):
        sums = list(sums)
        for j in range(2):
            here = slice(8 * j, 8 * j + 8)
            for s in range(batch):
                x = x0 + s
                tile = raws[j][:, s * 128 : s * 128 + 128]
                for b in range(BANDS):
                    total = sums[j * BANDS + b]
                    mid_ref[0, b, x, here, :] = jnp.exp2(total * rates[b])
                    sums[j * BANDS + b] = total + softplus(tile[8 * b : 8 * b + 8])
                for k in range(BANDS, BANDS + 3):
                    mid_ref[0, k, x, here, :] = pl.reciprocal(
                        1.0 + jnp.exp2(tile[8 * k : 8 * k + 8]), approx=True)
                mid_ref[0, BANDS + 3, x, here, :] = softplus(tile[8 * BANDS + 24 : 8 * BANDS + 32])
        return tuple(sums)

    zero = jnp.zeros((8, 128), F32)
    sums = (zero,) * (2 * BANDS)
    count = cells_x // batch
    hidden, raws = {}, {}
    for t in range(count + unroll):
        if t < count:
            hidden[t] = layer_one(t * batch)
        if unroll == 2 and 1 <= t <= count:
            raws[t - 1] = layer_two(hidden.pop(t - 1))
        if t >= unroll:
            if unroll == 1:
                raws[t - 1] = layer_two(hidden.pop(t - 1))
            sums = finish((t - unroll) * batch, raws.pop(t - unroll), sums)
    select = one_hot((8, 256), iota((8, 256), 0) == 3).astype(BF16)
    for j in range(2):
        for b in range(BANDS):
            sum_ref[b, 8 * j : 8 * j + 8, :] = sums[j * BANDS + b]
        here = slice(8 * j, 8 * j + 8)
        kappa = mid_ref[0, BANDS + 3, :, here, :].reshape(8 * cells_x, 128)
        both = jnp.concatenate(split(kappa), axis=1)
        occlusion = jnp.dot(both, tri_ref[...], preferred_element_type=F32)
        weight = jnp.exp2(occlusion * fade) * (1.0 - jnp.exp2(kappa * fade))
        mid_ref[0, BANDS + 3, :, here, :] = weight.reshape(cells_x, 8, 128)
        dep_ref[j] = lax.dot_general(select, both, (((1,), (1,)), ((), ())),
                                     preferred_element_type=F32) * (1.0 / total_z)


def back_kernel(total_x, unroll, mid_ref, inc_ref, dep_ref, depth_ref, mix_ref,
                light_ref, img_ref, prod_ref):
    cells_x = light_ref.shape[1]
    select = one_hot((8, 768), iota((8, 768), 0) == iota((8, 768), 1) // 256).astype(BF16)
    for j in range(2):
        here = slice(8 * j, 8 * j + 8)
        gains = []
        for b in range(BANDS):
            fade = jnp.exp2(inc_ref[b, here] * (depth_ref[b] * (-LOG2E / total_x)))
            gains.append([fade * mix_ref[k, b] for k in range(3)])

        def two(i, carry):
            products = [[], [], []]
            for x in (2 * i, 2 * i + 1):
                bands = [mid_ref[0, b, x, here, :] for b in range(BANDS)]
                weight = mid_ref[0, BANDS + 3, x, here, :]
                for k in range(3):
                    total = bands[0] * gains[0][k]
                    for b in range(1, BANDS):
                        total = total + bands[b] * gains[b][k]
                    light = total * mid_ref[0, BANDS + k, x, here, :]
                    light_ref[k, x, here, :] = light
                    products[k].append(light * weight)
            rows = pl.ds(pl.multiple_of(i * 16, 16), 16)
            for k in range(3):
                high, low = split(jnp.concatenate(products[k], axis=0))
                prod_ref[rows, 256 * k : 256 * k + 128] = high
                prod_ref[rows, 256 * k + 128 : 256 * k + 256] = low
            return carry

        lax.fori_loop(0, cells_x // 2, two, 0, unroll=unroll)
        img_ref[j] = lax.dot_general(select, prod_ref[...], (((1,), (1,)), ((), ())),
                                     preferred_element_type=F32) + dep_ref[j]


def front(features, w_in, b_in, w_out, b_out, band_depth, total_x, total_z, first, rows_y):
    _, cells_x, _, cells_z = features.shape
    skip = first // SLAB

    def small(*shape):
        return pl.BlockSpec(shape, lambda i: (0,) * len(shape))

    return pl.pallas_call(
        functools.partial(front_kernel, total_x, total_z, 4, 1),
        grid=(rows_y // SLAB,),
        in_specs=[
            pl.BlockSpec((FEATS, cells_x, SLAB, cells_z), lambda i: (0, 0, i + skip, 0)),
            small(FEATS, UNITS), small(1, UNITS), small(OUTS, UNITS), small(1, OUTS),
            pl.BlockSpec(memory_space=pltpu.SMEM),
        ],
        out_specs=[
            pl.BlockSpec((1, OUTS, cells_x, SLAB, cells_z), lambda i: (i, 0, 0, 0, 0)),
            pl.BlockSpec((BANDS, SLAB, cells_z), lambda i: (0, i, 0)),
            pl.BlockSpec((2, 8, 256), lambda i: (i, 0, 0)),
        ],
        out_shape=[
            jax.ShapeDtypeStruct((rows_y // SLAB, OUTS, cells_x, SLAB, cells_z), F32),
            jax.ShapeDtypeStruct((BANDS, rows_y, cells_z), F32),
            jax.ShapeDtypeStruct((rows_y // 8, 8, 256), F32),
        ],
        scratch_shapes=[
            pltpu.VMEM((SLAB * UNITS, 208), BF16),
            pltpu.VMEM((OUTS * 8, 400), BF16),
            pltpu.VMEM((256, 128), BF16),
        ],
        compiler_params=pltpu.CompilerParams(vmem_limit_bytes=30 << 20),
        name="front",
    )(*(pltpu.with_memory_space_constraint(value, pltpu.HBM)
        for value in (features, w_in.T, b_in[None], w_out, b_out[None])), band_depth)


def back(mid, incoming, dep, band_depth, band_mix, light, total_x, first, whole_y):
    slabs, _, cells_x, _, cells_z = mid.shape
    skip = first // SLAB
    operands = [mid, incoming, dep, band_depth, band_mix]
    in_specs = [
        pl.BlockSpec((1, OUTS, cells_x, SLAB, cells_z), lambda i: (i, 0, 0, 0, 0)),
        pl.BlockSpec((BANDS, SLAB, cells_z), lambda i: (0, i, 0)),
        pl.BlockSpec((2, 8, 256), lambda i: (i, 0, 0)),
        pl.BlockSpec(memory_space=pltpu.SMEM),
        pl.BlockSpec(memory_space=pltpu.SMEM),
    ]
    kernel = functools.partial(back_kernel, total_x, 4)
    aliases = {}
    if light is not None:
        operands.append(light)
        in_specs.append(pl.BlockSpec(memory_space=pl.ANY))
        aliases = {len(operands) - 1: 0}
        inner = kernel

        def kernel(*refs):
            inner(*refs[:5], *refs[6:])

    return pl.pallas_call(
        kernel,
        grid=(slabs,),
        in_specs=in_specs,
        out_specs=[
            pl.BlockSpec((3, cells_x, SLAB, cells_z), lambda i: (0, 0, i + skip, 0)),
            pl.BlockSpec((2, 8, 256), lambda i: (i, 0, 0)),
        ],
        out_shape=[
            jax.ShapeDtypeStruct((3, cells_x, whole_y, cells_z), F32),
            jax.ShapeDtypeStruct((2 * slabs, 8, 256), F32),
        ],
        scratch_shapes=[pltpu.VMEM((256, 768), BF16)],
        input_output_aliases=aliases,
        compiler_params=pltpu.CompilerParams(vmem_limit_bytes=30 << 20),
        name="back",
    )(*operands)


def swap(value, axis, partner):
    return lax.ppermute(value, axis, [(i, partner(i)) for i in range(lax.axis_size(axis))])


def across(i, bit):
    return i ^ 1 if bit == 0 else 3 - i


def scan_x(total):
    half = BANDS // 2
    me = lax.axis_index("gx")
    core, place = me % 2, (me // 2 % 4, me // 8)
    low, high = total[:half], total[half:]
    keep = jnp.where(core == 0, low, high)
    got = swap(jnp.where(core == 0, high, low), "gx", lambda i: i ^ 1)
    total = keep + got
    before = jnp.zeros_like(total)
    for axis in range(2):
        for bit in range(2):
            def partner(i):
                if axis == 0:
                    return i // 8 * 8 + across(i // 2 % 4, bit) * 2 + i % 2
                return across(i // 8, bit) * 8 + i % 8
            other = swap(total, "gx", partner)
            before = before + jnp.where(place[axis] >> bit & 1, other, 0.0)
            total = total + other
    mine = before + jnp.where(core == 0, 0.0, got)
    theirs = swap(before + jnp.where(core == 0, keep, 0.0), "gx", lambda i: i ^ 1)
    return jnp.concatenate([jnp.where(core == 0, mine, theirs), jnp.where(core == 0, theirs, mine)], axis=0)


def composite(parts, cells_x):
    ndev = lax.axis_size("gz")
    me = lax.axis_index("gz")
    slabs = parts.shape[0]
    parts = parts.reshape(ndev, slabs // ndev, 8, parts.shape[-1])
    held = []
    for apart in range(ndev):
        piece = lax.dynamic_index_in_dim(parts, (me + apart) % ndev, 0, keepdims=False)[:, :4]
        if apart:
            piece = lax.ppermute(piece, "gz", [(i, (i + apart) % ndev) for i in range(ndev)])
        held.append((piece, (me - apart) % ndev))
    colour = 0.0
    depth = 0.0
    for piece, source in held:
        ahead = 0.0
        for other, origin in held:
            if other is not piece:
                ahead = ahead + jnp.where(origin < source, other[:, 3:], 0.0)
        colour = colour + jnp.exp(-ahead) * piece[:, :3]
        depth = depth + piece[:, 3:]
    image = jnp.concatenate([colour, 1.0 - jnp.exp(-depth)], axis=1)
    image = image.reshape(slabs // ndev, 4, cells_x, 8)
    return image.transpose(1, 2, 0, 3).reshape(4, cells_x, slabs // ndev * 8)


def body(features, w_in, b_in, w_out, b_out, band_depth, band_mix):
    cells_x = features.shape[1]
    total_x = cells_x * lax.axis_size("gx")
    total_z = features.shape[3] * lax.axis_size("gz")
    rows_y = features.shape[2]
    size = rows_y // CHUNKS
    pieces = [
        front(features, w_in, b_in, w_out, b_out, band_depth, total_x, total_z, c * size, size)
        for c in range(CHUNKS)
    ]
    incoming = [scan_x(piece[1]) for piece in pieces]
    light, parts = None, []
    for c, (mid, _, dep) in enumerate(pieces):
        light, part = back(mid, incoming[c], dep, band_depth, band_mix, light, total_x, c * size, rows_y)
        parts.append(part)
    parts = jnp.concatenate(parts, axis=0)
    return light, composite(parts, cells_x)


def solution(mesh):
    in_specs = (P(None, "gx", None, "gz"), P(), P(), P(), P(), P(), P())
    out_specs = (P(None, "gx", None, "gz"), P(None, "gx", "gz"))
    return jax.shard_map(body, mesh=mesh, in_specs=in_specs, out_specs=out_specs, check_vma=False)
```

```python
import functools
import math

import jax
import jax.numpy as jnp
from jax import lax
from jax.experimental import pallas as pl
from jax.experimental.pallas import tpu as pltpu
from jax.sharding import PartitionSpec as P

BANDS = 8
HALF = BANDS // 2
UNITS = 16
FEATS = 4
OUTS = 12
SLAB = 16
LOG2E = math.log2(math.e)
F32 = jnp.float32
BF16 = jnp.bfloat16


def iota(shape, dim):
    return lax.broadcasted_iota(jnp.int32, shape, dim)


def split(value):
    high = value.astype(BF16)
    return high, (value - high.astype(F32)).astype(BF16)


def exact_dot(a, b):
    return jnp.dot(a, b, precision=lax.Precision.HIGHEST, preferred_element_type=F32)


def one_hot(shape, condition):
    return jnp.where(condition, jnp.ones(shape, F32), jnp.zeros(shape, F32))


def bias_columns(column):
    rows = column.shape[0]
    high = column.astype(BF16).astype(F32)
    rest = column - high
    middle = rest.astype(BF16).astype(F32)
    low = rest - middle
    lane = iota((rows, 16), 1)
    zero = jnp.zeros((rows, 16), F32)
    return jnp.where(
        lane == 0, high, jnp.where(lane == 1, middle, jnp.where(lane == 2, low, zero))
    ).astype(BF16)


def build_first(w_in, b_in):
    rows, cols = SLAB * UNITS, FEATS * SLAB
    pick = one_hot((rows, UNITS), iota((rows, UNITS), 0) % UNITS == iota((rows, UNITS), 1))
    spread = one_hot((FEATS, cols), iota((FEATS, cols), 1) // SLAB == iota((FEATS, cols), 0))
    full = exact_dot(exact_dot(pick, w_in), spread)
    full = jnp.where(iota((rows, cols), 0) // UNITS == iota((rows, cols), 1) % SLAB, full, 0.0)
    high, low = split(full)
    bias = bias_columns(jnp.sum(pick * b_in, axis=1, keepdims=True))
    return high, low, bias


def build_second(w_out, b_out):
    rows, cols = OUTS * 8, 8 * UNITS
    pick = one_hot((rows, OUTS), iota((rows, OUTS), 0) // 8 == iota((rows, OUTS), 1))
    spread = one_hot((UNITS, cols), iota((UNITS, cols), 1) % UNITS == iota((UNITS, cols), 0))
    full = exact_dot(exact_dot(pick, w_out), spread)
    full = jnp.where(iota((rows, cols), 0) % 8 == iota((rows, cols), 1) // UNITS, full, 0.0)
    out = iota((rows, 1), 0) // 8
    scale = jnp.where((out >= BANDS) & (out < BANDS + 3), -LOG2E, 1.0)
    high, low = split(full * scale)
    bias = bias_columns(jnp.sum(pick * b_out, axis=1, keepdims=True) * scale)
    return high, low, bias


def softplus(x):
    return jnp.maximum(jnp.log(1.0 + jnp.exp(jnp.minimum(x, 80.0))), x)


def front_kernel(total_x, total_z, batch, unroll, f_ref, win_ref, bin_ref, wout_ref, bout_ref, depth_ref, core_ref,
                 mid_ref, send_ref, keep_ref, dep_ref, first_ref, second_ref, tri_ref):
    cells_x = f_ref.shape[1]
    step = pl.program_id(0)
    core = core_ref[0]

    @pl.when(step == 0)
    def _():
        high, low, bias = build_first(win_ref[...].T, bin_ref[...])
        first_ref[:, 0:64] = high
        first_ref[:, 64:128] = high
        first_ref[:, 128:192] = low
        first_ref[:, 192:208] = bias
        high, low, bias = build_second(wout_ref[...], bout_ref[...])
        second_ref[:, 0:128] = high
        second_ref[:, 128:256] = high
        second_ref[:, 256:384] = low
        second_ref[:, 384:400] = bias
        tri_ref[...] = one_hot((256, 128), iota((256, 128), 0) % 128 < iota((256, 128), 1)).astype(BF16)

    ones = jnp.ones((16, 128 * batch), BF16)
    rates = [depth_ref[b] * (-LOG2E / total_x) for b in range(BANDS)]
    fade = -LOG2E / total_z

    y0 = pl.multiple_of(step * SLAB, SLAB)

    def layer_one(x0):
        rows = jnp.concatenate(
            [jnp.concatenate([f_ref[c, x0 + s] for s in range(batch)], axis=1) for c in range(FEATS)], axis=0
        )
        high, low = split(rows)
        return jnp.dot(first_ref[...], jnp.concatenate([high, low, high, ones], axis=0),
                       preferred_element_type=F32)

    def layer_two(hidden):
        high, low = split(jnp.maximum(hidden, 0.0))
        raws = []
        for j in range(2):
            part = slice(j * 128, j * 128 + 128)
            raws.append(jnp.dot(second_ref[...],
                                jnp.concatenate([high[part], low[part], high[part], ones], axis=0),
                                preferred_element_type=F32))
        return raws

    lane = iota((8, 128), 1)
    each = 128 // (2 * cells_x)

    def finish(x0, raws, sums, depth):
        sums = list(sums)
        for j in range(2):
            here = pl.ds(pl.multiple_of(y0 + 8 * j, 8), 8)
            for s in range(batch):
                x = x0 + s
                tile = raws[j][:, s * 128 : s * 128 + 128]
                for b in range(BANDS):
                    total = sums[j * BANDS + b]
                    mid_ref[b, x, here, :] = jnp.exp2(total * rates[b])
                    sums[j * BANDS + b] = total + softplus(tile[8 * b : 8 * b + 8])
                for k in range(BANDS, BANDS + 3):
                    mid_ref[k, x, here, :] = pl.reciprocal(
                        1.0 + jnp.exp2(tile[8 * k : 8 * k + 8]), approx=True)
                kappa = softplus(tile[8 * BANDS + 24 : 8 * BANDS + 32])
                mid_ref[BANDS + 3, x, here, :] = kappa
                column = jnp.sum(kappa, axis=1, keepdims=True)
                depth = jnp.where(lane == (step % each * 2 + j) * cells_x + x, column, depth)
        return tuple(sums), depth

    zero = jnp.zeros((8, 128), F32)
    sums, depth = (zero,) * (2 * BANDS), zero
    count = cells_x // batch
    hidden, raws = {}, {}
    for t in range(count + unroll):
        if t < count:
            hidden[t] = layer_one(t * batch)
        if unroll == 2 and 1 <= t <= count:
            raws[t - 1] = layer_two(hidden.pop(t - 1))
        if t >= unroll:
            if unroll == 1:
                raws[t - 1] = layer_two(hidden.pop(t - 1))
            sums, depth = finish((t - unroll) * batch, raws.pop(t - unroll), sums, depth)
    for j in range(2):
        for b in range(HALF):
            low, high = sums[j * BANDS + b], sums[j * BANDS + HALF + b]
            send_ref[b, 8 * j : 8 * j + 8, :] = jnp.where(core == 0, high, low)
            keep_ref[b, 8 * j : 8 * j + 8, :] = jnp.where(core == 0, low, high)
        here = pl.ds(pl.multiple_of(y0 + 8 * j, 8), 8)
        kappa = mid_ref[BANDS + 3, :, here, :].reshape(8 * cells_x, 128)
        both = jnp.concatenate(split(kappa), axis=1)
        occlusion = jnp.dot(both, tri_ref[...], preferred_element_type=F32)
        weight = jnp.exp2(occlusion * fade) * (1.0 - jnp.exp2(kappa * fade))
        mid_ref[BANDS + 3, :, here, :] = weight.reshape(cells_x, 8, 128)
    depth = depth * (1.0 / total_z)

    @pl.when(step % each == 0)
    def _():
        dep_ref[0] = depth

    @pl.when(step % each != 0)
    def _():
        dep_ref[0] = dep_ref[0] + depth


def back_kernel(total_x, unroll, mid_ref, mine_ref, theirs_ref, dep_ref, depth_ref, core_ref, mix_ref,
                light_ref, *img_refs):
    cells_x = light_ref.shape[1]
    ndev = len(img_refs)
    each = pl.num_programs(0) // ndev
    step = pl.program_id(0)
    apart = (step // each - core_ref[5] + ndev) % ndev
    lane = iota((8, 128), 1)
    colours = (jnp.zeros((8, 128), F32),) * 3
    for j in range(2):
        here = slice(8 * j, 8 * j + 8)
        deep = pl.ds(pl.multiple_of(pl.program_id(0) * SLAB + 8 * j, 8), 8)
        gains = []
        for b in range(BANDS):
            mine, theirs = mine_ref[b % HALF, here], theirs_ref[b % HALF, here]
            before = jnp.where(core_ref[0] == b // HALF, mine, theirs)
            fade = jnp.exp2(before * (depth_ref[b] * (-LOG2E / total_x)))
            gains.append([fade * mix_ref[k, b] for k in range(3)])
        first = (step % each * 2 + j) * cells_x

        def one(x, colours):
            bands = [mid_ref[b, x, deep, :] for b in range(BANDS)]
            weight = mid_ref[BANDS + 3, x, deep, :]
            place = lane == first + x
            result = []
            for k in range(3):
                total = bands[0] * gains[0][k]
                for b in range(1, BANDS):
                    total = total + bands[b] * gains[b][k]
                light = total * mid_ref[BANDS + k, x, deep, :]
                light_ref[k, x, here, :] = light
                column = jnp.sum(light * weight, axis=1, keepdims=True)
                result.append(jnp.where(place, column, colours[k]))
            return tuple(result)

        colours = lax.fori_loop(0, cells_x, one, colours, unroll=unroll)
    for other in range(ndev):
        @pl.when((apart == other) & (step % each == 0))
        def _():
            for k in range(3):
                img_refs[other][k] = colours[k]
            img_refs[other][3] = dep_ref[0]

        @pl.when((apart == other) & (step % each != 0))
        def _():
            for k in range(3):
                img_refs[other][k] = img_refs[other][k] + colours[k]


def front(features, w_in, b_in, w_out, b_out, band_depth, place, total_x, total_z, first, rows_y):
    _, cells_x, _, cells_z = features.shape
    skip = first // SLAB
    each = 128 // (2 * cells_x)

    whole = pl.BlockSpec(memory_space=pltpu.VMEM)

    def small(*shape):
        return pl.BlockSpec(shape, lambda i: (0,) * len(shape))

    return pl.pallas_call(
        functools.partial(front_kernel, total_x, total_z, 2, 2),
        grid=(rows_y // SLAB,),
        in_specs=[
            pl.BlockSpec((FEATS, cells_x, SLAB, cells_z), lambda i: (0, 0, i + skip, 0)),
            small(FEATS, UNITS), small(1, UNITS), small(OUTS, UNITS), small(1, OUTS),
            pl.BlockSpec(memory_space=pltpu.SMEM),
            pl.BlockSpec(memory_space=pltpu.SMEM),
        ],
        out_specs=[
            whole,
            pl.BlockSpec((HALF, SLAB, cells_z), lambda i: (0, i, 0)),
            pl.BlockSpec((HALF, SLAB, cells_z), lambda i: (0, i, 0)),
            pl.BlockSpec((1, 8, 128), lambda i: (i // each, 0, 0)),
        ],
        out_shape=[
            pltpu.MemorySpace.VMEM((OUTS, cells_x, rows_y, cells_z), F32),
            jax.ShapeDtypeStruct((HALF, rows_y, cells_z), F32),
            jax.ShapeDtypeStruct((HALF, rows_y, cells_z), F32),
            jax.ShapeDtypeStruct((rows_y // SLAB // each, 8, 128), F32),
        ],
        scratch_shapes=[
            pltpu.VMEM((SLAB * UNITS, 208), BF16),
            pltpu.VMEM((OUTS * 8, 400), BF16),
            pltpu.VMEM((256, 128), BF16),
        ],
        compiler_params=pltpu.CompilerParams(vmem_limit_bytes=16 << 20),
        name="front",
    )(*(pltpu.with_memory_space_constraint(value, pltpu.HBM)
        for value in (features, w_in.T, b_in[None], w_out, b_out[None])), band_depth, place)


def back(mid, incoming, dep, band_depth, place, band_mix, total_x, ndev):
    _, cells_x, rows_y, cells_z = mid.shape
    slabs = rows_y // SLAB
    each = slabs // ndev
    scalar = pl.BlockSpec(memory_space=pltpu.SMEM)
    whole = pl.BlockSpec(memory_space=pltpu.VMEM)
    return pl.pallas_call(
        functools.partial(back_kernel, total_x, cells_x),
        grid=(slabs,),
        in_specs=[
            whole,
            pl.BlockSpec((HALF, SLAB, cells_z), lambda i: (0, i, 0)),
            pl.BlockSpec((HALF, SLAB, cells_z), lambda i: (0, i, 0)),
            pl.BlockSpec((1, 8, 128), lambda i: (i // each, 0, 0)),
            scalar, scalar, scalar,
        ],
        out_specs=[pl.BlockSpec((3, cells_x, SLAB, cells_z), lambda i: (0, 0, i, 0))] + [whole] * ndev,
        out_shape=[jax.ShapeDtypeStruct((3, cells_x, rows_y, cells_z), F32)]
        + [jax.ShapeDtypeStruct((4, 8, 128), F32)] * ndev,
        compiler_params=pltpu.CompilerParams(vmem_limit_bytes=16 << 20),
        name="back",
    )(pltpu.with_memory_space_constraint(mid, pltpu.VMEM), *incoming, dep, band_depth, place, band_mix)


def swap(value, axis, partner):
    return lax.ppermute(value, axis, [(i, partner(i)) for i in range(lax.axis_size(axis))])


def across(i, bit):
    return i ^ 1 if bit == 0 else 3 - i


def small_kernel(body, arrays, place, outputs):
    whole = pl.BlockSpec(memory_space=pltpu.VMEM)
    shape = arrays[0].shape

    def kernel(place_ref, *refs):
        where = [place_ref[i] for i in range(6)]
        for band in range(shape[0]):
            values = [ref[band] for ref in refs[: len(arrays)]]
            for ref, value in zip(refs[len(arrays) :], body(where, *values), strict=True):
                ref[band] = value

    return pl.pallas_call(
        kernel,
        in_specs=[pl.BlockSpec(memory_space=pltpu.SMEM)] + [whole] * len(arrays),
        out_specs=[whole] * outputs,
        out_shape=[jax.ShapeDtypeStruct(shape, F32)] * outputs,
        compiler_params=pltpu.CompilerParams(vmem_limit_bytes=4 << 20),
        name="combine",
    )(place, *arrays)


def scan_x(send, keep, place):
    got = swap(send, "gx", lambda i: i ^ 1)
    (total,) = small_kernel(lambda where, a, b: [a + b], [keep, got], place, 1)
    before = None
    for stage in range(4):
        axis, bit = divmod(stage, 2)

        def partner(i):
            if axis == 0:
                return i // 8 * 8 + across(i // 2 % 4, bit) * 2 + i % 2
            return across(i // 8, bit) * 8 + i % 8

        other = swap(total, "gx", partner)

        def merge(where, total, other, before=0.0):
            return [total + other, before + jnp.where(where[1 + stage] == 1, other, 0.0)]

        def last(where, other, before, keep, got):
            before = before + jnp.where(where[1 + stage] == 1, other, 0.0)
            return [before + jnp.where(where[0] == 0, 0.0, got), before + jnp.where(where[0] == 0, keep, 0.0)]

        if stage < 3:
            total, before = small_kernel(merge, [total, other] + ([before] if stage else []), place, 2)
        else:
            mine, theirs = small_kernel(last, [other, before, keep, got], place, 2)
    return mine, swap(theirs, "gx", lambda i: i ^ 1)


def compose_kernel(place_ref, *refs):
    pieces, out_ref = refs[:-1], refs[-1]
    ndev = len(pieces)
    origin = [(place_ref[5] - apart + ndev) % ndev for apart in range(ndev)]
    depths = [piece[3] for piece in pieces]
    totals = [jnp.zeros_like(depths[0])] * 3
    for i in range(ndev):
        ahead = jnp.zeros_like(depths[0])
        for j in range(ndev):
            if j != i:
                ahead = ahead + jnp.where(origin[j] < origin[i], depths[j], 0.0)
        through = jnp.exp(-ahead)
        totals = [total + through * pieces[i][k] for k, total in enumerate(totals)]
    for k in range(3):
        out_ref[k] = totals[k]
    out_ref[3] = 1.0 - jnp.exp(-sum(depths[1:], depths[0]))


def composite(pieces, place, cells_x):
    ndev = len(pieces)
    held = [
        lax.ppermute(piece, "gz", [(i, (i + apart) % ndev) for i in range(ndev)]) if apart else piece
        for apart, piece in enumerate(pieces)
    ]
    whole = pl.BlockSpec(memory_space=pltpu.VMEM)
    image = pl.pallas_call(
        compose_kernel,
        in_specs=[pl.BlockSpec(memory_space=pltpu.SMEM)] + [whole] * ndev,
        out_specs=whole,
        out_shape=jax.ShapeDtypeStruct(pieces[0].shape, F32),
        compiler_params=pltpu.CompilerParams(vmem_limit_bytes=4 << 20),
        name="compose",
    )(place, *held)
    image = image.reshape(4, 8, 128 // cells_x, cells_x)
    return image.transpose(0, 3, 2, 1).reshape(4, cells_x, -1)


def body(features, w_in, b_in, w_out, b_out, band_depth, band_mix):
    cells_x = features.shape[1]
    total_x = cells_x * lax.axis_size("gx")
    total_z = features.shape[3] * lax.axis_size("gz")
    rows_y = features.shape[2]
    me = lax.axis_index("gx")
    place = jnp.stack([me % 2, me // 2 % 2, me // 4 % 2, me // 8 % 2, me // 16 % 2,
                       lax.axis_index("gz")]).astype(jnp.int32)
    mid, send, keep, dep = front(
        features, w_in, b_in, w_out, b_out, band_depth, place, total_x, total_z, 0, rows_y)
    incoming = scan_x(send, keep, place)
    light, *pieces = back(mid, incoming, dep, band_depth, place, band_mix, total_x, lax.axis_size("gz"))
    return light, composite(pieces, place, cells_x)


def solution(mesh):
    in_specs = (P(None, "gx", None, "gz"), P(), P(), P(), P(), P(), P())
    out_specs = (P(None, "gx", None, "gz"), P(None, "gx", "gz"))
    return jax.shard_map(body, mesh=mesh, in_specs=in_specs, out_specs=out_specs, check_vma=False)
```

```python
import functools
import math

import jax
import jax.numpy as jnp
from jax import lax
from jax.experimental import pallas as pl
from jax.experimental.pallas import tpu as pltpu
from jax.sharding import PartitionSpec as P

BANDS = 8
HALF = BANDS // 2
PIECES = 2
EACH = HALF // PIECES
UNITS = 16
FEATS = 4
OUTS = 12
SLAB = 16
LOG2E = math.log2(math.e)
F32 = jnp.float32
BF16 = jnp.bfloat16


def iota(shape, dim):
    return lax.broadcasted_iota(jnp.int32, shape, dim)


def split(value):
    high = value.astype(BF16)
    return high, (value - high.astype(F32)).astype(BF16)


def exact_dot(a, b):
    return jnp.dot(a, b, precision=lax.Precision.HIGHEST, preferred_element_type=F32)


def one_hot(shape, condition):
    return jnp.where(condition, jnp.ones(shape, F32), jnp.zeros(shape, F32))


def bias_columns(column):
    rows = column.shape[0]
    high = column.astype(BF16).astype(F32)
    rest = column - high
    middle = rest.astype(BF16).astype(F32)
    low = rest - middle
    lane = iota((rows, 16), 1)
    zero = jnp.zeros((rows, 16), F32)
    return jnp.where(
        lane == 0, high, jnp.where(lane == 1, middle, jnp.where(lane == 2, low, zero))
    ).astype(BF16)


def build_first(w_in, b_in):
    rows, cols = SLAB * UNITS, FEATS * SLAB
    pick = one_hot((rows, UNITS), iota((rows, UNITS), 0) % UNITS == iota((rows, UNITS), 1))
    spread = one_hot((FEATS, cols), iota((FEATS, cols), 1) // SLAB == iota((FEATS, cols), 0))
    full = exact_dot(exact_dot(pick, w_in), spread)
    full = jnp.where(iota((rows, cols), 0) // UNITS == iota((rows, cols), 1) % SLAB, full, 0.0)
    high, low = split(full)
    bias = bias_columns(jnp.sum(pick * b_in, axis=1, keepdims=True))
    return high, low, bias


def build_second(w_out, b_out):
    rows, cols = OUTS * 8, 8 * UNITS
    pick = one_hot((rows, OUTS), iota((rows, OUTS), 0) // 8 == iota((rows, OUTS), 1))
    spread = one_hot((UNITS, cols), iota((UNITS, cols), 1) % UNITS == iota((UNITS, cols), 0))
    full = exact_dot(exact_dot(pick, w_out), spread)
    full = jnp.where(iota((rows, cols), 0) % 8 == iota((rows, cols), 1) // UNITS, full, 0.0)
    out = iota((rows, 1), 0) // 8
    scale = jnp.where((out >= BANDS) & (out < BANDS + 3), -LOG2E, 1.0)
    high, low = split(full * scale)
    bias = bias_columns(jnp.sum(pick * b_out, axis=1, keepdims=True) * scale)
    return high, low, bias


def softplus(x):
    return jnp.maximum(jnp.log(1.0 + jnp.exp(jnp.minimum(x, 80.0))), x)


def front_kernel(total_x, total_z, batch, unroll, f_ref, win_ref, bin_ref, wout_ref, bout_ref, depth_ref, core_ref,
                 mid_ref, *rest):
    cells_x = f_ref.shape[1]
    send_refs, keep_refs = rest[:PIECES], rest[PIECES : 2 * PIECES]
    dep_ref, first_ref, second_ref, tri_ref = rest[2 * PIECES :]
    step = pl.program_id(0)
    core = core_ref[0]

    @pl.when(step == 0)
    def _():
        high, low, bias = build_first(win_ref[...].T, bin_ref[...])
        first_ref[:, 0:64] = high
        first_ref[:, 64:128] = high
        first_ref[:, 128:192] = low
        first_ref[:, 192:208] = bias
        high, low, bias = build_second(wout_ref[...], bout_ref[...])
        second_ref[:, 0:128] = high
        second_ref[:, 128:256] = high
        second_ref[:, 256:384] = low
        second_ref[:, 384:400] = bias
        tri_ref[...] = one_hot((256, 128), iota((256, 128), 0) % 128 < iota((256, 128), 1)).astype(BF16)

    ones = jnp.ones((16, 128 * batch), BF16)
    rates = [depth_ref[b] * (-LOG2E / total_x) for b in range(BANDS)]
    fade = -LOG2E / total_z

    y0 = pl.multiple_of(step * SLAB, SLAB)

    def layer_one(x0):
        rows = jnp.concatenate(
            [jnp.concatenate([f_ref[c, x0 + s] for s in range(batch)], axis=1) for c in range(FEATS)], axis=0
        )
        high, low = split(rows)
        return jnp.dot(first_ref[...], jnp.concatenate([high, low, high, ones], axis=0),
                       preferred_element_type=F32)

    def layer_two(hidden):
        high, low = split(jnp.maximum(hidden, 0.0))
        raws = []
        for j in range(2):
            part = slice(j * 128, j * 128 + 128)
            raws.append(jnp.dot(second_ref[...],
                                jnp.concatenate([high[part], low[part], high[part], ones], axis=0),
                                preferred_element_type=F32))
        return raws

    lane = iota((8, 128), 1)
    each = 128 // (2 * cells_x)

    def finish(x0, raws, sums, depth):
        sums = list(sums)
        for j in range(2):
            here = pl.ds(pl.multiple_of(y0 + 8 * j, 8), 8)
            for s in range(batch):
                x = x0 + s
                tile = raws[j][:, s * 128 : s * 128 + 128]
                for b in range(BANDS):
                    total = sums[j * BANDS + b]
                    mid_ref[b, x, here, :] = jnp.exp2(total * rates[b])
                    sums[j * BANDS + b] = total + softplus(tile[8 * b : 8 * b + 8])
                for k in range(BANDS, BANDS + 3):
                    mid_ref[k, x, here, :] = pl.reciprocal(
                        1.0 + jnp.exp2(tile[8 * k : 8 * k + 8]), approx=True)
                kappa = softplus(tile[8 * BANDS + 24 : 8 * BANDS + 32])
                mid_ref[BANDS + 3, x, here, :] = kappa
                column = jnp.sum(kappa, axis=1, keepdims=True)
                depth = jnp.where(lane == (step % each * 2 + j) * cells_x + x, column, depth)
        return tuple(sums), depth

    zero = jnp.zeros((8, 128), F32)
    sums, depth = (zero,) * (2 * BANDS), zero
    count = cells_x // batch
    hidden, raws = {}, {}
    for t in range(count + unroll):
        if t < count:
            hidden[t] = layer_one(t * batch)
        if unroll == 2 and 1 <= t <= count:
            raws[t - 1] = layer_two(hidden.pop(t - 1))
        if t >= unroll:
            if unroll == 1:
                raws[t - 1] = layer_two(hidden.pop(t - 1))
            sums, depth = finish((t - unroll) * batch, raws.pop(t - unroll), sums, depth)
    for j in range(2):
        for b in range(HALF):
            low, high = sums[j * BANDS + b], sums[j * BANDS + HALF + b]
            send_refs[b // EACH][b % EACH, 8 * j : 8 * j + 8, :] = jnp.where(core == 0, high, low)
            keep_refs[b // EACH][b % EACH, 8 * j : 8 * j + 8, :] = jnp.where(core == 0, low, high)
        here = pl.ds(pl.multiple_of(y0 + 8 * j, 8), 8)
        kappa = mid_ref[BANDS + 3, :, here, :].reshape(8 * cells_x, 128)
        both = jnp.concatenate(split(kappa), axis=1)
        occlusion = jnp.dot(both, tri_ref[...], preferred_element_type=F32)
        weight = jnp.exp2(occlusion * fade) * (1.0 - jnp.exp2(kappa * fade))
        mid_ref[BANDS + 3, :, here, :] = weight.reshape(cells_x, 8, 128)
    depth = depth * (1.0 / total_z)

    @pl.when(step % each == 0)
    def _():
        dep_ref[0] = depth

    @pl.when(step % each != 0)
    def _():
        dep_ref[0] = dep_ref[0] + depth


def back_kernel(total_x, unroll, mid_ref, *rest):
    mine_refs, theirs_refs = rest[:PIECES], rest[PIECES : 2 * PIECES]
    dep_ref, depth_ref, core_ref, mix_ref, light_ref, *img_refs = rest[2 * PIECES :]
    cells_x = light_ref.shape[1]
    ndev = len(img_refs)
    each = pl.num_programs(0) // ndev
    step = pl.program_id(0)
    apart = (step // each - core_ref[5] + ndev) % ndev
    lane = iota((8, 128), 1)
    colours = (jnp.zeros((8, 128), F32),) * 3
    for j in range(2):
        here = slice(8 * j, 8 * j + 8)
        deep = pl.ds(pl.multiple_of(pl.program_id(0) * SLAB + 8 * j, 8), 8)
        gains = []
        for b in range(BANDS):
            piece, band = divmod(b % HALF, EACH)
            mine, theirs = mine_refs[piece][band, here], theirs_refs[piece][band, here]
            before = jnp.where(core_ref[0] == b // HALF, mine, theirs)
            fade = jnp.exp2(before * (depth_ref[b] * (-LOG2E / total_x)))
            gains.append([fade * mix_ref[k, b] for k in range(3)])
        first = (step % each * 2 + j) * cells_x

        def one(x, colours):
            bands = [mid_ref[b, x, deep, :] for b in range(BANDS)]
            weight = mid_ref[BANDS + 3, x, deep, :]
            place = lane == first + x
            result = []
            for k in range(3):
                total = bands[0] * gains[0][k]
                for b in range(1, BANDS):
                    total = total + bands[b] * gains[b][k]
                light = total * mid_ref[BANDS + k, x, deep, :]
                light_ref[k, x, here, :] = light
                column = jnp.sum(light * weight, axis=1, keepdims=True)
                result.append(jnp.where(place, column, colours[k]))
            return tuple(result)

        colours = lax.fori_loop(0, cells_x, one, colours, unroll=unroll)
    for other in range(ndev):
        @pl.when((apart == other) & (step % each == 0))
        def _():
            for k in range(3):
                img_refs[other][k] = colours[k]
            img_refs[other][3] = dep_ref[0]

        @pl.when((apart == other) & (step % each != 0))
        def _():
            for k in range(3):
                img_refs[other][k] = img_refs[other][k] + colours[k]


def front(features, w_in, b_in, w_out, b_out, band_depth, place, total_x, total_z, first, rows_y):
    _, cells_x, _, cells_z = features.shape
    skip = first // SLAB
    each = 128 // (2 * cells_x)

    whole = pl.BlockSpec(memory_space=pltpu.VMEM)

    def small(*shape):
        return pl.BlockSpec(shape, lambda i: (0,) * len(shape))

    return pl.pallas_call(
        functools.partial(front_kernel, total_x, total_z, 2, 2),
        grid=(rows_y // SLAB,),
        in_specs=[
            pl.BlockSpec((FEATS, cells_x, SLAB, cells_z), lambda i: (0, 0, i + skip, 0)),
            small(FEATS, UNITS), small(1, UNITS), small(OUTS, UNITS), small(1, OUTS),
            pl.BlockSpec(memory_space=pltpu.SMEM),
            pl.BlockSpec(memory_space=pltpu.SMEM),
        ],
        out_specs=[
            whole,
            *[pl.BlockSpec((EACH, SLAB, cells_z), lambda i: (0, i, 0))] * (2 * PIECES),
            pl.BlockSpec((1, 8, 128), lambda i: (i // each, 0, 0)),
        ],
        out_shape=[
            pltpu.MemorySpace.VMEM((OUTS, cells_x, rows_y, cells_z), F32),
            *[jax.ShapeDtypeStruct((EACH, rows_y, cells_z), F32)] * (2 * PIECES),
            jax.ShapeDtypeStruct((rows_y // SLAB // each, 8, 128), F32),
        ],
        scratch_shapes=[
            pltpu.VMEM((SLAB * UNITS, 208), BF16),
            pltpu.VMEM((OUTS * 8, 400), BF16),
            pltpu.VMEM((256, 128), BF16),
        ],
        compiler_params=pltpu.CompilerParams(vmem_limit_bytes=16 << 20),
        name="front",
    )(*(pltpu.with_memory_space_constraint(value, pltpu.HBM)
        for value in (features, w_in.T, b_in[None], w_out, b_out[None])), band_depth, place)


def back(mid, incoming, dep, band_depth, place, band_mix, total_x, ndev):
    _, cells_x, rows_y, cells_z = mid.shape
    slabs = rows_y // SLAB
    each = slabs // ndev
    scalar = pl.BlockSpec(memory_space=pltpu.SMEM)
    whole = pl.BlockSpec(memory_space=pltpu.VMEM)
    return pl.pallas_call(
        functools.partial(back_kernel, total_x, cells_x),
        grid=(slabs,),
        in_specs=[
            whole,
            *[pl.BlockSpec((EACH, SLAB, cells_z), lambda i: (0, i, 0))] * (2 * PIECES),
            pl.BlockSpec((1, 8, 128), lambda i: (i // each, 0, 0)),
            scalar, scalar, scalar,
        ],
        out_specs=[pl.BlockSpec((3, cells_x, SLAB, cells_z), lambda i: (0, 0, i, 0))] + [whole] * ndev,
        out_shape=[jax.ShapeDtypeStruct((3, cells_x, rows_y, cells_z), F32)]
        + [jax.ShapeDtypeStruct((4, 8, 128), F32)] * ndev,
        compiler_params=pltpu.CompilerParams(vmem_limit_bytes=16 << 20),
        name="back",
    )(pltpu.with_memory_space_constraint(mid, pltpu.VMEM), *incoming, dep, band_depth, place, band_mix)


def swap(value, axis, partner):
    return lax.ppermute(value, axis, [(i, partner(i)) for i in range(lax.axis_size(axis))])


def across(i, bit):
    return i ^ 1 if bit == 0 else 3 - i


def small_kernel(body, arrays, place, outputs):
    whole = pl.BlockSpec(memory_space=pltpu.VMEM)
    shape = arrays[0].shape

    def kernel(place_ref, *refs):
        where = [place_ref[i] for i in range(6)]
        for band in range(shape[0]):
            values = [ref[band] for ref in refs[: len(arrays)]]
            for ref, value in zip(refs[len(arrays) :], body(where, *values), strict=True):
                ref[band] = value

    return pl.pallas_call(
        kernel,
        in_specs=[pl.BlockSpec(memory_space=pltpu.SMEM)] + [whole] * len(arrays),
        out_specs=[whole] * outputs,
        out_shape=[jax.ShapeDtypeStruct(shape, F32)] * outputs,
        compiler_params=pltpu.CompilerParams(vmem_limit_bytes=4 << 20),
        name="combine",
    )(place, *arrays)


def scan_x(send, keep, place):
    got = swap(send, "gx", lambda i: i ^ 1)
    (total,) = small_kernel(lambda where, a, b: [a + b], [keep, got], place, 1)
    before = None
    for stage in range(4):
        axis, bit = divmod(stage, 2)

        def partner(i):
            if axis == 0:
                return i // 8 * 8 + across(i // 2 % 4, bit) * 2 + i % 2
            return across(i // 8, bit) * 8 + i % 8

        other = swap(total, "gx", partner)

        def merge(where, total, other, before=0.0):
            return [total + other, before + jnp.where(where[1 + stage] == 1, other, 0.0)]

        def last(where, other, before, keep, got):
            before = before + jnp.where(where[1 + stage] == 1, other, 0.0)
            return [before + jnp.where(where[0] == 0, 0.0, got), before + jnp.where(where[0] == 0, keep, 0.0)]

        if stage < 3:
            total, before = small_kernel(merge, [total, other] + ([before] if stage else []), place, 2)
        else:
            mine, theirs = small_kernel(last, [other, before, keep, got], place, 2)
    return mine, swap(theirs, "gx", lambda i: i ^ 1)


def compose_kernel(place_ref, *refs):
    pieces, out_ref = refs[:-1], refs[-1]
    ndev = len(pieces)
    origin = [(place_ref[5] - apart + ndev) % ndev for apart in range(ndev)]
    depths = [piece[3] for piece in pieces]
    totals = [jnp.zeros_like(depths[0])] * 3
    for i in range(ndev):
        ahead = jnp.zeros_like(depths[0])
        for j in range(ndev):
            if j != i:
                ahead = ahead + jnp.where(origin[j] < origin[i], depths[j], 0.0)
        through = jnp.exp(-ahead)
        totals = [total + through * pieces[i][k] for k, total in enumerate(totals)]
    for k in range(3):
        out_ref[k] = totals[k]
    out_ref[3] = 1.0 - jnp.exp(-sum(depths[1:], depths[0]))


def composite(pieces, place, cells_x):
    ndev = len(pieces)
    held = [
        lax.ppermute(piece, "gz", [(i, (i + apart) % ndev) for i in range(ndev)]) if apart else piece
        for apart, piece in enumerate(pieces)
    ]
    whole = pl.BlockSpec(memory_space=pltpu.VMEM)
    image = pl.pallas_call(
        compose_kernel,
        in_specs=[pl.BlockSpec(memory_space=pltpu.SMEM)] + [whole] * ndev,
        out_specs=whole,
        out_shape=jax.ShapeDtypeStruct(pieces[0].shape, F32),
        compiler_params=pltpu.CompilerParams(vmem_limit_bytes=4 << 20),
        name="compose",
    )(place, *held)
    image = image.reshape(4, 8, 128 // cells_x, cells_x)
    return image.transpose(0, 3, 2, 1).reshape(4, cells_x, -1)


def body(features, w_in, b_in, w_out, b_out, band_depth, band_mix):
    cells_x = features.shape[1]
    total_x = cells_x * lax.axis_size("gx")
    total_z = features.shape[3] * lax.axis_size("gz")
    rows_y = features.shape[2]
    me = lax.axis_index("gx")
    place = jnp.stack([me % 2, me // 2 % 2, me // 4 % 2, me // 8 % 2, me // 16 % 2,
                       lax.axis_index("gz")]).astype(jnp.int32)
    mid, *sums, dep = front(
        features, w_in, b_in, w_out, b_out, band_depth, place, total_x, total_z, 0, rows_y)
    scanned = [scan_x(sums[i], sums[PIECES + i], place) for i in range(PIECES)]
    incoming = [mine for mine, _ in scanned] + [theirs for _, theirs in scanned]
    light, *pieces = back(mid, incoming, dep, band_depth, place, band_mix, total_x, lax.axis_size("gz"))
    return light, composite(pieces, place, cells_x)


def solution(mesh):
    in_specs = (P(None, "gx", None, "gz"), P(), P(), P(), P(), P(), P())
    out_specs = (P(None, "gx", None, "gz"), P(None, "gx", "gz"))
    return jax.shard_map(body, mesh=mesh, in_specs=in_specs, out_specs=out_specs, check_vma=False)
```

```python
import functools
import math

import jax
import jax.numpy as jnp
from jax import lax
from jax.experimental import pallas as pl
from jax.experimental.pallas import tpu as pltpu
from jax.sharding import PartitionSpec as P

BANDS = 8
HALF = BANDS // 2
PIECES = 2
EACH = HALF // PIECES
UNITS = 16
FEATS = 4
OUTS = 12
SLAB = 16
LOG2E = math.log2(math.e)
F32 = jnp.float32
BF16 = jnp.bfloat16


def iota(shape, dim):
    return lax.broadcasted_iota(jnp.int32, shape, dim)


def split(value):
    high = value.astype(BF16)
    return high, (value - high.astype(F32)).astype(BF16)


def exact_dot(a, b):
    return jnp.dot(a, b, precision=lax.Precision.HIGHEST, preferred_element_type=F32)


def one_hot(shape, condition):
    return jnp.where(condition, jnp.ones(shape, F32), jnp.zeros(shape, F32))


def bias_columns(column):
    rows = column.shape[0]
    high = column.astype(BF16).astype(F32)
    rest = column - high
    middle = rest.astype(BF16).astype(F32)
    low = rest - middle
    lane = iota((rows, 16), 1)
    zero = jnp.zeros((rows, 16), F32)
    return jnp.where(
        lane == 0, high, jnp.where(lane == 1, middle, jnp.where(lane == 2, low, zero))
    ).astype(BF16)


def build_first(w_in, b_in):
    rows, cols = SLAB * UNITS, FEATS * SLAB
    pick = one_hot((rows, UNITS), iota((rows, UNITS), 0) % UNITS == iota((rows, UNITS), 1))
    spread = one_hot((FEATS, cols), iota((FEATS, cols), 1) // SLAB == iota((FEATS, cols), 0))
    full = exact_dot(exact_dot(pick, w_in), spread)
    full = jnp.where(iota((rows, cols), 0) // UNITS == iota((rows, cols), 1) % SLAB, full, 0.0)
    high, low = split(full)
    bias = bias_columns(jnp.sum(pick * b_in, axis=1, keepdims=True))
    return high, low, bias


def build_second(w_out, b_out):
    rows, cols = OUTS * 8, 8 * UNITS
    pick = one_hot((rows, OUTS), iota((rows, OUTS), 0) // 8 == iota((rows, OUTS), 1))
    spread = one_hot((UNITS, cols), iota((UNITS, cols), 1) % UNITS == iota((UNITS, cols), 0))
    full = exact_dot(exact_dot(pick, w_out), spread)
    full = jnp.where(iota((rows, cols), 0) % 8 == iota((rows, cols), 1) // UNITS, full, 0.0)
    out = iota((rows, 1), 0) // 8
    scale = jnp.where((out >= BANDS) & (out < BANDS + 3), -LOG2E, 1.0)
    high, low = split(full * scale)
    bias = bias_columns(jnp.sum(pick * b_out, axis=1, keepdims=True) * scale)
    return high, low, bias


def softplus(x):
    return jnp.maximum(jnp.log(1.0 + jnp.exp(jnp.minimum(x, 80.0))), x)


def front_kernel(total_x, total_z, batch, unroll, f_ref, win_ref, bin_ref, wout_ref, bout_ref, depth_ref, core_ref,
                 mid_ref, *rest):
    cells_x = f_ref.shape[1]
    send_refs, keep_refs = rest[:PIECES], rest[PIECES : 2 * PIECES]
    dep_ref, flag_ref, first_ref, second_ref, tri_ref = rest[2 * PIECES :]
    step = pl.program_id(0)
    core = core_ref[0]

    @pl.when(step == 0)
    def _():
        for i in range(6):
            flag_ref[i] = jnp.full((8, 128), core_ref[i], jnp.int32).astype(F32)
        high, low, bias = build_first(win_ref[...].T, bin_ref[...])
        first_ref[:, 0:64] = high
        first_ref[:, 64:128] = high
        first_ref[:, 128:192] = low
        first_ref[:, 192:208] = bias
        high, low, bias = build_second(wout_ref[...], bout_ref[...])
        second_ref[:, 0:128] = high
        second_ref[:, 128:256] = high
        second_ref[:, 256:384] = low
        second_ref[:, 384:400] = bias
        tri_ref[...] = one_hot((256, 128), iota((256, 128), 0) % 128 < iota((256, 128), 1)).astype(BF16)

    ones = jnp.ones((16, 128 * batch), BF16)
    rates = [depth_ref[b] * (-LOG2E / total_x) for b in range(BANDS)]
    fade = -LOG2E / total_z

    y0 = pl.multiple_of(step * SLAB, SLAB)

    def layer_one(x0):
        rows = jnp.concatenate(
            [jnp.concatenate([f_ref[c, x0 + s] for s in range(batch)], axis=1) for c in range(FEATS)], axis=0
        )
        high, low = split(rows)
        return jnp.dot(first_ref[...], jnp.concatenate([high, low, high, ones], axis=0),
                       preferred_element_type=F32)

    def layer_two(hidden):
        high, low = split(jnp.maximum(hidden, 0.0))
        raws = []
        for j in range(2):
            part = slice(j * 128, j * 128 + 128)
            raws.append(jnp.dot(second_ref[...],
                                jnp.concatenate([high[part], low[part], high[part], ones], axis=0),
                                preferred_element_type=F32))
        return raws

    lane = iota((8, 128), 1)
    each = 128 // (2 * cells_x)

    def finish(x0, raws, sums, depth):
        sums = list(sums)
        for j in range(2):
            here = pl.ds(pl.multiple_of(y0 + 8 * j, 8), 8)
            for s in range(batch):
                x = x0 + s
                tile = raws[j][:, s * 128 : s * 128 + 128]
                for b in range(BANDS):
                    total = sums[j * BANDS + b]
                    mid_ref[b, x, here, :] = jnp.exp2(total * rates[b])
                    sums[j * BANDS + b] = total + softplus(tile[8 * b : 8 * b + 8])
                for k in range(BANDS, BANDS + 3):
                    mid_ref[k, x, here, :] = pl.reciprocal(
                        1.0 + jnp.exp2(tile[8 * k : 8 * k + 8]), approx=True)
                kappa = softplus(tile[8 * BANDS + 24 : 8 * BANDS + 32])
                mid_ref[BANDS + 3, x, here, :] = kappa
                column = jnp.sum(kappa, axis=1, keepdims=True)
                depth = jnp.where(lane == (step % each * 2 + j) * cells_x + x, column, depth)
        return tuple(sums), depth

    zero = jnp.zeros((8, 128), F32)
    sums, depth = (zero,) * (2 * BANDS), zero
    count = cells_x // batch
    hidden, raws = {}, {}
    for t in range(count + unroll):
        if t < count:
            hidden[t] = layer_one(t * batch)
        if unroll == 2 and 1 <= t <= count:
            raws[t - 1] = layer_two(hidden.pop(t - 1))
        if t >= unroll:
            if unroll == 1:
                raws[t - 1] = layer_two(hidden.pop(t - 1))
            sums, depth = finish((t - unroll) * batch, raws.pop(t - unroll), sums, depth)
    for j in range(2):
        for b in range(HALF):
            low, high = sums[j * BANDS + b], sums[j * BANDS + HALF + b]
            send_refs[b // EACH][b % EACH, 8 * j : 8 * j + 8, :] = jnp.where(core == 0, high, low)
            keep_refs[b // EACH][b % EACH, 8 * j : 8 * j + 8, :] = jnp.where(core == 0, low, high)
        here = pl.ds(pl.multiple_of(y0 + 8 * j, 8), 8)
        kappa = mid_ref[BANDS + 3, :, here, :].reshape(8 * cells_x, 128)
        both = jnp.concatenate(split(kappa), axis=1)
        occlusion = jnp.dot(both, tri_ref[...], preferred_element_type=F32)
        weight = jnp.exp2(occlusion * fade) * (1.0 - jnp.exp2(kappa * fade))
        mid_ref[BANDS + 3, :, here, :] = weight.reshape(cells_x, 8, 128)
    depth = depth * (1.0 / total_z)

    @pl.when(step % each == 0)
    def _():
        dep_ref[0] = depth

    @pl.when(step % each != 0)
    def _():
        dep_ref[0] = dep_ref[0] + depth


def back_kernel(total_x, unroll, mid_ref, *rest):
    mine_refs, theirs_refs = rest[:PIECES], rest[PIECES : 2 * PIECES]
    dep_ref, depth_ref, core_ref, mix_ref, light_ref, *img_refs = rest[2 * PIECES :]
    cells_x = light_ref.shape[1]
    ndev = len(img_refs)
    each = pl.num_programs(0) // ndev
    step = pl.program_id(0)
    apart = (step // each - core_ref[5] + ndev) % ndev
    lane = iota((8, 128), 1)
    colours = (jnp.zeros((8, 128), F32),) * 3
    for j in range(2):
        here = slice(8 * j, 8 * j + 8)
        deep = pl.ds(pl.multiple_of(pl.program_id(0) * SLAB + 8 * j, 8), 8)
        gains = []
        for b in range(BANDS):
            piece, band = divmod(b % HALF, EACH)
            mine, theirs = mine_refs[piece][band, here], theirs_refs[piece][band, here]
            before = jnp.where(core_ref[0] == b // HALF, mine, theirs)
            fade = jnp.exp2(before * (depth_ref[b] * (-LOG2E / total_x)))
            gains.append([fade * mix_ref[k, b] for k in range(3)])
        first = (step % each * 2 + j) * cells_x

        def one(x, colours):
            bands = [mid_ref[b, x, deep, :] for b in range(BANDS)]
            weight = mid_ref[BANDS + 3, x, deep, :]
            place = lane == first + x
            result = []
            for k in range(3):
                total = bands[0] * gains[0][k]
                for b in range(1, BANDS):
                    total = total + bands[b] * gains[b][k]
                light = total * mid_ref[BANDS + k, x, deep, :]
                light_ref[k, x, here, :] = light
                column = jnp.sum(light * weight, axis=1, keepdims=True)
                result.append(jnp.where(place, column, colours[k]))
            return tuple(result)

        colours = lax.fori_loop(0, cells_x, one, colours, unroll=unroll)
    for other in range(ndev):
        @pl.when((apart == other) & (step % each == 0))
        def _():
            for k in range(3):
                img_refs[other][k] = colours[k]
            img_refs[other][3] = dep_ref[0]

        @pl.when((apart == other) & (step % each != 0))
        def _():
            for k in range(3):
                img_refs[other][k] = img_refs[other][k] + colours[k]


def front(features, w_in, b_in, w_out, b_out, band_depth, place, total_x, total_z, first, rows_y):
    _, cells_x, _, cells_z = features.shape
    skip = first // SLAB
    each = 128 // (2 * cells_x)

    whole = pl.BlockSpec(memory_space=pltpu.VMEM)

    def small(*shape):
        return pl.BlockSpec(shape, lambda i: (0,) * len(shape))

    return pl.pallas_call(
        functools.partial(front_kernel, total_x, total_z, 2, 2),
        grid=(rows_y // SLAB,),
        in_specs=[
            pl.BlockSpec((FEATS, cells_x, SLAB, cells_z), lambda i: (0, 0, i + skip, 0)),
            small(FEATS, UNITS), small(1, UNITS), small(OUTS, UNITS), small(1, OUTS),
            pl.BlockSpec(memory_space=pltpu.SMEM),
            pl.BlockSpec(memory_space=pltpu.SMEM),
        ],
        out_specs=[
            whole,
            *[pl.BlockSpec((EACH, SLAB, cells_z), lambda i: (0, i, 0))] * (2 * PIECES),
            pl.BlockSpec((1, 8, 128), lambda i: (i // each, 0, 0)),
            whole,
        ],
        out_shape=[
            pltpu.MemorySpace.VMEM((OUTS, cells_x, rows_y, cells_z), F32),
            *[jax.ShapeDtypeStruct((EACH, rows_y, cells_z), F32)] * (2 * PIECES),
            jax.ShapeDtypeStruct((rows_y // SLAB // each, 8, 128), F32),
            jax.ShapeDtypeStruct((6, 8, 128), F32),
        ],
        scratch_shapes=[
            pltpu.VMEM((SLAB * UNITS, 208), BF16),
            pltpu.VMEM((OUTS * 8, 400), BF16),
            pltpu.VMEM((256, 128), BF16),
        ],
        compiler_params=pltpu.CompilerParams(vmem_limit_bytes=16 << 20),
        name="front",
    )(*(pltpu.with_memory_space_constraint(value, pltpu.HBM)
        for value in (features, w_in.T, b_in[None], w_out, b_out[None])), band_depth, place)


def back(mid, incoming, dep, band_depth, place, band_mix, total_x, ndev):
    _, cells_x, rows_y, cells_z = mid.shape
    slabs = rows_y // SLAB
    each = slabs // ndev
    scalar = pl.BlockSpec(memory_space=pltpu.SMEM)
    whole = pl.BlockSpec(memory_space=pltpu.VMEM)
    return pl.pallas_call(
        functools.partial(back_kernel, total_x, cells_x),
        grid=(slabs,),
        in_specs=[
            whole,
            *[pl.BlockSpec((EACH, SLAB, cells_z), lambda i: (0, i, 0))] * (2 * PIECES),
            pl.BlockSpec((1, 8, 128), lambda i: (i // each, 0, 0)),
            scalar, scalar, scalar,
        ],
        out_specs=[pl.BlockSpec((3, cells_x, SLAB, cells_z), lambda i: (0, 0, i, 0))] + [whole] * ndev,
        out_shape=[jax.ShapeDtypeStruct((3, cells_x, rows_y, cells_z), F32)]
        + [jax.ShapeDtypeStruct((4, 8, 128), F32)] * ndev,
        compiler_params=pltpu.CompilerParams(vmem_limit_bytes=16 << 20),
        name="back",
    )(pltpu.with_memory_space_constraint(mid, pltpu.VMEM), *incoming, dep, band_depth, place, band_mix)


def swap(value, axis, partner):
    return lax.ppermute(value, axis, [(i, partner(i)) for i in range(lax.axis_size(axis))])


def across(i, bit):
    return i ^ 1 if bit == 0 else 3 - i


def small_kernel(body, arrays, place, outputs):
    whole = pl.BlockSpec(memory_space=pltpu.VMEM)
    shape = arrays[0].shape

    def kernel(flag_ref, *refs):
        where = [flag_ref[i, 0:1] for i in range(5)]
        for band in range(shape[0]):
            values = [ref[band] for ref in refs[: len(arrays)]]
            for ref, value in zip(refs[len(arrays) :], body(where, *values), strict=True):
                ref[band] = value

    return pl.pallas_call(
        kernel,
        in_specs=[whole] * (1 + len(arrays)),
        out_specs=[whole] * outputs,
        out_shape=[jax.ShapeDtypeStruct(shape, F32)] * outputs,
        compiler_params=pltpu.CompilerParams(vmem_limit_bytes=4 << 20),
        name="combine",
    )(place, *arrays)


def scan_x(send, keep, place):
    got = swap(send, "gx", lambda i: i ^ 1)
    (total,) = small_kernel(lambda where, a, b: [a + b], [keep, got], place, 1)
    before = None
    for stage in range(4):
        axis, bit = divmod(stage, 2)

        def partner(i):
            if axis == 0:
                return i // 8 * 8 + across(i // 2 % 4, bit) * 2 + i % 2
            return across(i // 8, bit) * 8 + i % 8

        other = swap(total, "gx", partner)

        def merge(where, total, other, before=0.0):
            return [total + other, before + other * where[1 + stage]]

        def last(where, other, before, keep, got):
            before = before + other * where[1 + stage]
            return [before + got * where[0], before + keep * (1.0 - where[0])]

        if stage < 3:
            total, before = small_kernel(merge, [total, other] + ([before] if stage else []), place, 2)
        else:
            mine, theirs = small_kernel(last, [other, before, keep, got], place, 2)
    return mine, swap(theirs, "gx", lambda i: i ^ 1)


def compose_kernel(flag_ref, *refs):
    pieces, out_ref = refs[:-1], refs[-1]
    ndev = len(pieces)
    origin = [flag_ref[5] - apart for apart in range(ndev)]
    origin = [jnp.where(value < 0.0, value + ndev, value) for value in origin]
    depths = [piece[3] for piece in pieces]
    totals = [jnp.zeros_like(depths[0])] * 3
    for i in range(ndev):
        ahead = jnp.zeros_like(depths[0])
        for j in range(ndev):
            if j != i:
                ahead = ahead + jnp.where(origin[j] < origin[i], depths[j], 0.0)
        through = jnp.exp(-ahead)
        totals = [total + through * pieces[i][k] for k, total in enumerate(totals)]
    for k in range(3):
        out_ref[k] = totals[k]
    out_ref[3] = 1.0 - jnp.exp(-sum(depths[1:], depths[0]))


def composite(pieces, flags, cells_x):
    ndev = len(pieces)
    held = [
        lax.ppermute(piece, "gz", [(i, (i + apart) % ndev) for i in range(ndev)]) if apart else piece
        for apart, piece in enumerate(pieces)
    ]
    whole = pl.BlockSpec(memory_space=pltpu.VMEM)
    image = pl.pallas_call(
        compose_kernel,
        in_specs=[whole] * (1 + ndev),
        out_specs=whole,
        out_shape=jax.ShapeDtypeStruct(pieces[0].shape, F32),
        compiler_params=pltpu.CompilerParams(vmem_limit_bytes=4 << 20),
        name="compose",
    )(flags, *held)
    image = image.reshape(4, 8, 128 // cells_x, cells_x)
    return image.transpose(0, 3, 2, 1).reshape(4, cells_x, -1)


def body(features, w_in, b_in, w_out, b_out, band_depth, band_mix):
    cells_x = features.shape[1]
    total_x = cells_x * lax.axis_size("gx")
    total_z = features.shape[3] * lax.axis_size("gz")
    rows_y = features.shape[2]
    me = lax.axis_index("gx")
    place = jnp.stack([me % 2, me // 2 % 2, me // 4 % 2, me // 8 % 2, me // 16 % 2,
                       lax.axis_index("gz")]).astype(jnp.int32)
    mid, *sums, dep, flags = front(
        features, w_in, b_in, w_out, b_out, band_depth, place, total_x, total_z, 0, rows_y)
    scanned = [scan_x(sums[i], sums[PIECES + i], flags) for i in range(PIECES)]
    incoming = [mine for mine, _ in scanned] + [theirs for _, theirs in scanned]
    light, *pieces = back(mid, incoming, dep, band_depth, place, band_mix, total_x, lax.axis_size("gz"))
    return light, composite(pieces, flags, cells_x)


def solution(mesh):
    in_specs = (P(None, "gx", None, "gz"), P(), P(), P(), P(), P(), P())
    out_specs = (P(None, "gx", None, "gz"), P(None, "gx", "gz"))
    return jax.shard_map(body, mesh=mesh, in_specs=in_specs, out_specs=out_specs, check_vma=False)
```
